32 devices in a mesh: expert: 4 (over z), rep: 4 (over y, core), hid: 2 (over x).
Axes of the slice: x: 2, y: 2, z: 4, core: 2. Of those that a mesh axis runs over, the one named last changes fastest.
Arguments:
- tokens: bfloat16 [64, 6144], P(('expert', 'hid'), 'rep'), may hold values from -6 to 6
- norm_gain: float32 [6144], P('rep'), may hold values from 0.25 to 1.75
- expert_ids: int32 [64, 2], P(('expert', 'hid')), may hold values from 0 to 3, as said below
- slot_ids: int32 [64, 2], P(('expert', 'hid')), may hold values from 0 to 4, as said below
- w_gate: bfloat16 [4, 6144, 8192], P('expert', 'rep', 'hid'), may hold values from -0.078125 to 0.078125
- w_up: bfloat16 [4, 6144, 8192], P('expert', 'rep', 'hid'), may hold values from -0.078125 to 0.078125
- grad_gate: bfloat16 [4, 40, 8192], P('expert', None, 'hid'), may hold values from -1.1953125 to 1.1953125
- grad_up: bfloat16 [4, 40, 8192], P('expert', None, 'hid'), may hold values from -1.1953125 to 1.1953125
Outputs:
- grad_w_gate: bfloat16 [4, 6144, 8192], P('expert', 'rep', 'hid')
- grad_w_up: bfloat16 [4, 6144, 8192], P('expert', 'rep', 'hid')
- grad_tokens: bfloat16 [64, 6144], P(('expert', 'hid'), 'rep')
The draws below stay inside these ranges and needn't reach their ends.
Inputs may be any that keep to these rules, and one draw needn't show every extreme that they name: `expert_ids`: each token names two different experts; among the 8 tokens of one block, no expert is named more than 5 times and some expert exactly 5 times. Within one block of 8 tokens, the pairs (expert_ids[t, k], slot_ids[t, k]) are all different.
All inputs are finite; a program needn't handle non-finite values.
Results may differ from the reference program's by a relative error of at most 0.0049.
Values may be sent and summed in bfloat16 or wider, within the bound.
A program may use at most 128 MiB of HBM per device.

```python
import jax
import jax.numpy as jnp
from jax import lax

D = 6144
FF = 8192
TOK_DEV = 8
EXPERTS = 4
HSPLIT = 2
CAP = 5
ROWS = 40
TOKENS = 64


def routing_plan(key):
    blocks = TOKENS // TOK_DEV
    slots_all = EXPERTS * CAP
    dropped = slots_all - 2 * TOK_DEV
    block_keys = jax.random.split(jax.random.fold_in(key, 101), blocks)

    def one_block(block_key):
        key_full, key_score, key_order, key_flip = jax.random.split(block_key, 4)
        full_expert = jax.random.randint(key_full, (), 0, EXPERTS)
        position = jnp.arange(slots_all, dtype=jnp.int32)
        scores = jax.random.permutation(key_score, slots_all).astype(jnp.int32)
        scores = jnp.where(position // CAP == full_expert, slots_all + position, scores)
        ranked = jnp.argsort(scores)
        kept = jnp.sort(ranked[dropped:]).astype(jnp.int32)
        order = jax.random.permutation(key_order, TOK_DEV)
        first = kept[:TOK_DEV][order]
        second = kept[TOK_DEV:][order]
        flipped = jax.random.randint(key_flip, (TOK_DEV,), 0, 2) == 1
        leading = jnp.where(flipped, second, first)
        trailing = jnp.where(flipped, first, second)
        return jnp.stack([leading, trailing], axis=1)
    return jax.vmap(one_block)(block_keys).reshape(TOKENS, 2).astype(jnp.int32)


def draw_expert_ids(key, part):
    return routing_plan(key) // CAP


def draw_slot_ids(key, part):
    return routing_plan(key) % CAP


def with_spikes(array, rng, source, target, parts, factor):
    def block_of(axis_at):
        return (jnp.arange(array.shape[axis_at]) // (array.shape[axis_at] // parts)).reshape((-1,) + (1,) * (array.ndim - 1 - axis_at))

    one_side = jax.random.permutation(rng, parts)[block_of(target)]
    other_side = (block_of(target) + parts // 2) % parts
    return jnp.where((block_of(source) == one_side) | (block_of(source) == other_side), factor * array, array)


def steps_of(rng, shape, cuts, least, largest):
    def one(axis_at, blocks):
        steps = jax.random.uniform(jax.random.fold_in(jax.random.fold_in(rng, 6), axis_at), (blocks,), jnp.float32, least / len(cuts), largest / len(cuts))
        return jnp.repeat(jnp.exp(steps), shape[axis_at] // blocks).reshape((-1,) + (1,) * (len(shape) - axis_at - 1))

    loudness = one(*cuts[0])
    for cut in cuts[1:]:
        loudness = loudness * one(*cut)
    return loudness


def noise(rng, shape, width, most, cuts=(), kind=jnp.bfloat16):
    entries = width * jax.random.normal(rng, shape, jnp.float32)
    if cuts:
        entries = entries * steps_of(rng, shape, cuts, -0.22, 0.18)
    return jnp.clip(entries, -most, most).astype(kind)


def bell_draw_with(key, dims, width, limit, shards, heavy, kind=jnp.bfloat16):
    result = width * jax.random.normal(key, dims, jnp.float32)
    if shards:
        result = result * steps_of(key, dims, shards, -0.22, 0.18)
    return jnp.clip(with_spikes(result, jax.random.fold_in(key, 3), *heavy), -limit, limit).astype(kind)


def setup_inputs(seed: int = 0) -> dict:
    key_of = jax.random.split(jax.random.key(seed), 9)
    return {
        "tokens": noise(key_of[0], (TOKENS, D), 1.0, 6.0, ((0, 8), (1, 4))),
        "norm_gain": jnp.clip(1.0 + 0.15 * jax.random.normal(key_of[1], (D,), jnp.float32), 0.25, 1.75),
        "expert_ids": draw_expert_ids(jax.random.fold_in(key_of[8], 71), 0),
        "slot_ids": draw_slot_ids(jax.random.fold_in(key_of[8], 71), 0),
        "w_gate": noise(key_of[4], (EXPERTS, D, FF), D ** -0.5, 0.078125, ((0, 4), (1, 4), (2, 2))),
        "w_up": noise(key_of[5], (EXPERTS, D, FF), D ** -0.5, 0.078125, ((0, 4), (1, 4), (2, 2))),
        "grad_gate": bell_draw_with(key_of[6], (EXPERTS, ROWS, FF), 0.15, 1.1953125, ((0, 4), (2, 2)), (2, 1, 2, 2.0)),
        "grad_up": noise(key_of[7], (EXPERTS, ROWS, FF), 0.15, 1.1953125, ((0, 4), (2, 2))),
    }


def reference(tokens, norm_gain, expert_ids, slot_ids, w_gate, w_up, grad_gate, grad_up):
    values = tokens.astype(jnp.float32)
    inverse_rms = lax.rsqrt(lax.optimization_barrier(jnp.mean(values * values, axis=1, keepdims=True)) + 1e-05)
    scaled_in = values * inverse_rms
    normed = (scaled_in * norm_gain).astype(jnp.bfloat16)
    block_index = jnp.arange(TOKENS, dtype=jnp.int32) // TOK_DEV
    source_group = block_index // HSPLIT
    source_hid = block_index % HSPLIT
    row_base = (source_hid * EXPERTS + source_group) * CAP
    row_index = (row_base[:, None] + slot_ids).astype(jnp.int32)
    expert_rows = jnp.zeros((EXPERTS, ROWS, D), normed.dtype)
    for member in range(2):
        expert_rows = expert_rows.at[expert_ids[:, member], row_index[:, member]].set(normed)
    gate_list = []
    up_list = []
    row_list = []
    for expert in range(EXPERTS):
        gate_list.append(jnp.dot(expert_rows[expert].T, grad_gate[expert], preferred_element_type=jnp.float32).astype(jnp.bfloat16))
        up_list.append(jnp.dot(expert_rows[expert].T, grad_up[expert], preferred_element_type=jnp.float32).astype(jnp.bfloat16))
        summed = jnp.dot(grad_gate[expert], w_gate[expert].T, preferred_element_type=jnp.float32)
        summed = summed + jnp.dot(grad_up[expert], w_up[expert].T, preferred_element_type=jnp.float32)
        row_list.append(summed.astype(jnp.bfloat16))
    grad_w_gate = jnp.stack(gate_list)
    grad_w_up = jnp.stack(up_list)
    row_grads = jnp.stack(row_list)
    normed_grad = jnp.zeros((TOKENS, D), jnp.float32)
    for member in range(2):
        normed_grad = normed_grad + row_grads[expert_ids[:, member], row_index[:, member]].astype(jnp.float32)
    scaled = normed_grad * norm_gain
    dotted = lax.optimization_barrier(jnp.mean(scaled * scaled_in, axis=1, keepdims=True))
    grad_tokens = (inverse_rms * (scaled - scaled_in * dotted)).astype(jnp.bfloat16)
    return (grad_w_gate, grad_w_up, grad_tokens)
```

```python
import functools

import jax
import jax.numpy as jnp
from jax import lax
from jax.experimental import pallas as pl
from jax.experimental.pallas import tpu as pltpu
from jax.sharding import PartitionSpec as P

EPS = 1e-05
MESH = pl.DeviceIdType.MESH
F32 = jnp.float32
BF16 = jnp.bfloat16
MIB = 1024 * 1024


def divisor_up_to(size, most, step):
    best = size
    for width in range(step, most + 1, step):
        if size % width == 0:
            best = width
    return best


def exchange_kernel(
    sizes,
    tokens_ref,
    gain_ref,
    experts_ref,
    slots_ref,
    w_gate_ref,
    w_up_ref,
    gate_ref,
    up_ref,
    rows_t_ref,
    grad_tokens_ref,
    gate_buf,
    up_buf,
    gate_pad,
    up_pad,
    outgoing,
    arrived,
    back_out,
    back_in,
    sums,
    w_sem,
    sum_send,
    sum_recv,
    row_send,
    row_recv,
    back_send,
    back_recv,
):
    groups, reps, hids, slot_count, pad, chunk, per_send, sends, model = sizes
    blocks = groups * hids
    shift = pad.bit_length() - 1
    my_e = lax.axis_index("expert")
    my_r = lax.axis_index("rep")
    my_h = lax.axis_index("hid")
    me = my_h * groups + my_e
    chunks = per_send * sends
    block_tokens, feats = tokens_ref.shape
    slot_rows = gate_ref.shape[0]

    def weight_copies(c):
        rows = pl.ds(pl.multiple_of(c * chunk, chunk), chunk)
        return (
            pltpu.make_async_copy(w_gate_ref.at[rows, :], gate_buf.at[c], w_sem.at[0, c]),
            pltpu.make_async_copy(w_up_ref.at[rows, :], up_buf.at[c], w_sem.at[1, c]),
        )

    def start_weights(c, carry):
        for copy in weight_copies(c):
            copy.start()
        return carry

    lax.fori_loop(0, chunks, start_weights, 0)

    def block_at(step):
        other = lax.rem(me + step, blocks)
        return other, (lax.rem(other, groups), my_r, lax.div(other, groups))

    def rep_at(step):
        other = lax.rem(my_r + step, reps)
        return other, (my_e, other, my_h)

    barrier = pltpu.get_barrier_semaphore()

    def greet_rep(step, carry):
        pl.semaphore_signal(barrier, inc=1, device_id=rep_at(step)[1], device_id_type=MESH)
        return carry

    def greet_block(step, carry):
        pl.semaphore_signal(barrier, inc=1, device_id=block_at(step)[1], device_id_type=MESH)
        return carry

    lax.fori_loop(1, reps, greet_rep, 0)
    lax.fori_loop(1, blocks, greet_block, 0)

    def sum_copy(turn, step, sending):
        there, where = rep_at(step if sending else reps - step)
        slot = my_r if sending else there
        return pltpu.make_async_remote_copy(
            src_ref=sums.at[turn, my_r],
            dst_ref=sums.at[turn, slot],
            send_sem=sum_send.at[turn, step],
            recv_sem=sum_recv.at[turn, slot],
            device_id=where,
            device_id_type=MESH,
        )

    def send_sums(turn):
        def go(step, carry):
            sum_copy(turn, step, True).start()
            return carry

        lax.fori_loop(1, reps, go, 0)

    def wait_sums(turn):
        def go(step, carry):
            sum_copy(turn, step, False).wait_recv()
            return carry

        lax.fori_loop(1, reps, go, 0)
        return jnp.sum(sums[turn], axis=0)[:, :1]

    values = tokens_ref[...].astype(F32)
    sums[0, my_r] = jnp.broadcast_to(
        jnp.sum(values * values, axis=1, keepdims=True), (block_tokens, 128)
    )

    wide = blocks * pad
    padded_at = lax.broadcasted_iota(jnp.int32, (wide, slot_rows), 0)
    packed_at = lax.broadcasted_iota(jnp.int32, (wide, slot_rows), 1)
    slot_at = padded_at & (pad - 1)
    spread = (
        (packed_at == (padded_at >> shift) * slot_count + slot_at) & (slot_at < slot_count)
    ).astype(F32).astype(BF16)
    gate_pad[...] = jnp.dot(spread, gate_ref[...], preferred_element_type=F32).astype(BF16)
    up_pad[...] = jnp.dot(spread, up_ref[...], preferred_element_type=F32).astype(BF16)

    code = experts_ref[...] * pad + slots_ref[...]
    code_at = lax.broadcasted_iota(jnp.int32, (groups * pad, block_tokens), 0)
    onehot = ((code[0:1, :] == code_at) | (code[1:2, :] == code_at)).astype(F32)

    pl.semaphore_wait(barrier, reps + blocks - 2)
    send_sums(0)

    def back_copy(s, step, sending):
        there, where = block_at(step if sending else blocks - step)
        slot = me if sending else there
        return pltpu.make_async_remote_copy(
            src_ref=back_out.at[s, there],
            dst_ref=back_in.at[s, slot],
            send_sem=back_send.at[s, step],
            recv_sem=back_recv.at[s, slot],
            device_id=where,
            device_id_type=MESH,
        )

    contract_last = (((1,), (1,)), ((), ()))

    def back_part(s, carry):
        for part in range(per_send):
            c = s * per_send + part
            gate_copy, up_copy = weight_copies(c)
            gate_copy.wait()
            total = lax.dot_general(
                gate_pad[...], gate_buf[c], contract_last, preferred_element_type=F32
            )
            up_copy.wait()
            total = total + lax.dot_general(
                up_pad[...], up_buf[c], contract_last, preferred_element_type=F32
            )
            back_out[s, :, :, part * chunk : (part + 1) * chunk] = total.astype(BF16).reshape(
                blocks, pad, chunk
            )

        def go(step, inner):
            back_copy(s, step, True).start()
            return inner

        lax.fori_loop(1, blocks, go, 0)
        back_in[s, me] = back_out[s, me]
        return carry

    back_part(0, 0)

    gain = gain_ref[...]
    inverse_rms = lax.rsqrt(wait_sums(0) / model + EPS)
    scaled_in = values * inverse_rms
    normed = (scaled_in * gain).astype(BF16)
    outgoing[...] = (
        jnp.dot(onehot.astype(BF16), normed, preferred_element_type=F32)
        .astype(BF16)
        .reshape(groups, pad, feats)
    )

    def row_copy(step, sending):
        there, where = block_at(step if sending else blocks - step)
        slot = me if sending else there
        return pltpu.make_async_remote_copy(
            src_ref=outgoing.at[lax.rem(there, groups)],
            dst_ref=arrived.at[slot],
            send_sem=row_send.at[step],
            recv_sem=row_recv.at[slot],
            device_id=where,
            device_id_type=MESH,
        )

    def start_rows(step, carry):
        row_copy(step, True).start()
        return carry

    lax.fori_loop(1, blocks, start_rows, 0)
    arrived[me] = outgoing[my_e]

    lax.fori_loop(1, sends, back_part, 0)

    def wait_rows(step, carry):
        row_copy(step, False).wait_recv()
        return carry

    lax.fori_loop(1, blocks, wait_rows, 0)
    rows_t_ref[...] = lax.dot_general(
        arrived[...].reshape(wide, feats),
        spread,
        (((0,), (0,)), ((), ())),
        preferred_element_type=F32,
    ).astype(BF16)

    def wait_back(s, carry):
        def go(step, inner):
            back_copy(s, step, False).wait_recv()
            return inner

        return lax.fori_loop(1, blocks, go, carry)

    lax.fori_loop(0, sends, wait_back, 0)
    pick = jnp.concatenate([onehot] * hids, axis=0).astype(BF16)
    normed_grad = jnp.concatenate(
        [
            lax.dot_general(
                pick,
                back_in[s].reshape(wide, per_send * chunk),
                (((0,), (0,)), ((), ())),
                preferred_element_type=F32,
            )
            for s in range(sends)
        ],
        axis=1,
    )
    scaled = normed_grad * gain
    sums[1, my_r] = jnp.broadcast_to(
        jnp.sum(scaled * scaled_in, axis=1, keepdims=True), (block_tokens, 128)
    )
    send_sums(1)

    def sent_rows(step, carry):
        row_copy(step, True).wait_send()
        return carry

    def sent_back(s, carry):
        def go(step, inner):
            back_copy(s, step, True).wait_send()
            return inner

        return lax.fori_loop(1, blocks, go, carry)

    lax.fori_loop(1, blocks, sent_rows, 0)
    lax.fori_loop(0, sends, sent_back, 0)
    dotted = wait_sums(1) / model
    grad_tokens_ref[...] = (inverse_rms * (scaled - scaled_in * dotted)).astype(BF16)

    def sent_sums(step, carry):
        sum_copy(0, step, True).wait_send()
        sum_copy(1, step, True).wait_send()
        return carry

    lax.fori_loop(1, reps, sent_sums, 0)


def weight_grad_kernel(
    chunk, columns, rows_t_ref, gate_ref, up_ref, gate_out, up_out, gate_buf, up_buf, sem
):
    feats = rows_t_ref.shape[0]
    width = gate_ref.shape[1]

    def out_copies(c):
        rows = pl.ds(pl.multiple_of(c * chunk, chunk), chunk)
        return (
            pltpu.make_async_copy(gate_buf.at[c], gate_out.at[rows, :], sem.at[0, c]),
            pltpu.make_async_copy(up_buf.at[c], up_out.at[rows, :], sem.at[1, c]),
        )

    def one(c, carry):
        lhs = rows_t_ref[pl.ds(pl.multiple_of(c * chunk, chunk), chunk), :]
        copies = out_copies(c)
        for cot_ref, buf, copy in ((gate_ref, gate_buf, copies[0]), (up_ref, up_buf, copies[1])):
            for at in range(0, width, columns):
                buf[c, :, at : at + columns] = jnp.dot(
                    lhs, cot_ref[:, at : at + columns], preferred_element_type=F32
                ).astype(BF16)
            copy.start()
        return carry

    lax.fori_loop(0, feats // chunk, one, 0)

    def finish(c, carry):
        for copy in out_copies(c):
            copy.wait()
        return carry

    lax.fori_loop(0, feats // chunk, finish, 0)


def on_device(model, tokens, norm_gain, expert_ids, slot_ids, w_gate, w_up, grad_gate, grad_up):
    groups, reps, hids = (lax.axis_size(name) for name in ("expert", "rep", "hid"))
    blocks = groups * hids
    block_tokens, feats = tokens.shape
    slot_count = 5 * block_tokens // (2 * groups)
    pad = max(8, 1 << (slot_count - 1).bit_length())
    width = w_gate.shape[2]
    slot_rows = grad_gate.shape[1]
    chunk = divisor_up_to(feats, 256, 128)
    chunks = feats // chunk
    per_send = 2 if chunks % 2 == 0 else 1
    sends = chunks // per_send
    vmem = pl.BlockSpec(memory_space=pltpu.VMEM)
    hbm = pl.BlockSpec(memory_space=pl.ANY)
    wide = blocks * pad
    weight_bytes = feats * width * 2
    gate_cot = grad_gate[0]
    up_cot = grad_up[0]
    rows_t, grad_tokens = pl.pallas_call(
        functools.partial(
            exchange_kernel,
            (groups, reps, hids, slot_count, pad, chunk, per_send, sends, model),
        ),
        out_shape=(
            jax.ShapeDtypeStruct((feats, slot_rows), BF16),
            jax.ShapeDtypeStruct((block_tokens, feats), BF16),
        ),
        in_specs=[vmem, vmem, vmem, vmem, hbm, hbm, vmem, vmem],
        out_specs=(vmem, vmem),
        scratch_shapes=[
            pltpu.VMEM((chunks, chunk, width), BF16),
            pltpu.VMEM((chunks, chunk, width), BF16),
            pltpu.VMEM((wide, width), BF16),
            pltpu.VMEM((wide, width), BF16),
            pltpu.VMEM((groups, pad, feats), BF16),
            pltpu.VMEM((blocks, pad, feats), BF16),
            pltpu.VMEM((sends, blocks, pad, per_send * chunk), BF16),
            pltpu.VMEM((sends, blocks, pad, per_send * chunk), BF16),
            pltpu.VMEM((2, reps, block_tokens, 128), F32),
            pltpu.SemaphoreType.DMA((2, chunks)),
            pltpu.SemaphoreType.DMA((2, reps)),
            pltpu.SemaphoreType.DMA((2, reps)),
            pltpu.SemaphoreType.DMA((blocks,)),
            pltpu.SemaphoreType.DMA((blocks,)),
            pltpu.SemaphoreType.DMA((sends, blocks)),
            pltpu.SemaphoreType.DMA((sends, blocks)),
        ],
        compiler_params=pltpu.CompilerParams(
            collective_id=0, has_side_effects=True, vmem_limit_bytes=48 * MIB
        ),
        cost_estimate=pl.CostEstimate(
            flops=4 * wide * feats * width,
            bytes_accessed=2 * weight_bytes,
            transcendentals=0,
        ),
        name="rows_and_token_grads",
    )(
        tokens,
        norm_gain.reshape(1, feats),
        expert_ids.T,
        slot_ids.T,
        w_gate[0],
        w_up[0],
        gate_cot,
        up_cot,
    )
    new_gate, new_up = pl.pallas_call(
        functools.partial(weight_grad_kernel, chunk, divisor_up_to(width, 512, 128)),
        out_shape=(
            jax.ShapeDtypeStruct((feats, width), BF16),
            jax.ShapeDtypeStruct((feats, width), BF16),
        ),
        in_specs=[vmem, vmem, vmem],
        out_specs=(hbm, hbm),
        scratch_shapes=[
            pltpu.VMEM((chunks, chunk, width), BF16),
            pltpu.VMEM((chunks, chunk, width), BF16),
            pltpu.SemaphoreType.DMA((2, chunks)),
        ],
        compiler_params=pltpu.CompilerParams(vmem_limit_bytes=48 * MIB),
        cost_estimate=pl.CostEstimate(
            flops=4 * slot_rows * feats * width,
            bytes_accessed=2 * weight_bytes,
            transcendentals=0,
        ),
        name="weight_grads",
    )(rows_t, gate_cot, up_cot)
    return new_gate[None], new_up[None], grad_tokens


def solution(mesh):
    placed = (
        P(("expert", "hid"), "rep"),
        P("rep"),
        P(("expert", "hid"), None),
        P(("expert", "hid"), None),
        P("expert", "rep", "hid"),
        P("expert", "rep", "hid"),
        P("expert", None, "hid"),
        P("expert", None, "hid"),
    )

    def whole(tokens, *rest):
        return jax.shard_map(
            functools.partial(on_device, tokens.shape[1]),
            mesh=mesh,
            in_specs=placed,
            out_specs=(
                P("expert", "rep", "hid"),
                P("expert", "rep", "hid"),
                P(("expert", "hid"), "rep"),
            ),
            check_vma=False,
        )(tokens, *rest)

    return whole
```

```python
import functools

import jax
import jax.numpy as jnp
from jax import lax
from jax.experimental import pallas as pl
from jax.experimental.pallas import tpu as pltpu
from jax.sharding import PartitionSpec as P

EPS = 1e-05
MESH = pl.DeviceIdType.MESH
F32 = jnp.float32
BF16 = jnp.bfloat16
MIB = 1024 * 1024


def divisor_up_to(size, most, step):
    best = size
    for width in range(step, most + 1, step):
        if size % width == 0:
            best = width
    return best


def each(first, last, body):
    if last - first <= 8:
        for step in range(first, last):
            body(step)
    else:

        def go(step, carry):
            body(step)
            return carry

        lax.fori_loop(first, last, go, 0)


def exchange_kernel(
    sizes,
    tokens_hbm,
    gain_hbm,
    experts_hbm,
    slots_hbm,
    w_gate_ref,
    w_up_ref,
    gate_hbm,
    up_hbm,
    rows_t_ref,
    grad_tokens_ref,
    tokens_ref,
    gain_ref,
    experts_ref,
    slots_ref,
    gate_ref,
    up_ref,
    gate_buf,
    up_buf,
    gate_t,
    up_t,
    outgoing,
    arrived,
    back_out,
    back_in,
    sums,
    in_sem,
    w_sem,
    sum_send,
    sum_recv,
    row_send,
    row_recv,
    back_send,
    back_recv,
):
    groups, reps, hids, slot_count, pad, sends, cuts, model = sizes
    blocks = groups * hids
    shift = pad.bit_length() - 1
    my_e = lax.axis_index("expert")
    my_r = lax.axis_index("rep")
    my_h = lax.axis_index("hid")
    me = my_h * groups + my_e
    block_tokens, feats = tokens_ref.shape
    slot_rows = gate_ref.shape[0]
    part = feats // sends
    piece = gate_ref.shape[1] // cuts

    small = [
        pltpu.make_async_copy(src, dst, in_sem.at[i])
        for i, (src, dst) in enumerate(
            (
                (tokens_hbm, tokens_ref),
                (gate_hbm, gate_ref),
                (up_hbm, up_ref),
                (gain_hbm, gain_ref),
                (experts_hbm, experts_ref),
                (slots_hbm, slots_ref),
            )
        )
    ]
    for copy in small:
        copy.start()

    def weight_copies(s, k):
        at = (pl.ds(s * part, part), pl.ds(k * piece, piece))
        return (
            pltpu.make_async_copy(w_gate_ref.at[at], gate_buf.at[s, k], w_sem.at[0, s, k]),
            pltpu.make_async_copy(w_up_ref.at[at], up_buf.at[s, k], w_sem.at[1, s, k]),
        )

    for s in range(sends):
        for k in range(cuts):
            for copy in weight_copies(s, k):
                copy.start()

    def block_at(step):
        other = lax.rem(me + step, blocks)
        return other, (lax.rem(other, groups), my_r, lax.div(other, groups))

    def rep_at(step):
        other = lax.rem(my_r + step, reps)
        return other, (my_e, other, my_h)

    if blocks <= 9:
        block_list = [block_at(step) for step in range(blocks)]

        def block_at(step):
            return block_list[step]

    barrier = pltpu.get_barrier_semaphore()
    each(
        1,
        reps,
        lambda step: pl.semaphore_signal(
            barrier, inc=1, device_id=rep_at(step)[1], device_id_type=MESH
        ),
    )
    each(
        1,
        blocks,
        lambda step: pl.semaphore_signal(
            barrier, inc=1, device_id=block_at(step)[1], device_id_type=MESH
        ),
    )

    def sum_copy(turn, step, sending):
        there, where = rep_at(step if sending else reps - step)
        slot = my_r if sending else there
        return pltpu.make_async_remote_copy(
            src_ref=sums.at[turn, my_r],
            dst_ref=sums.at[turn, slot],
            send_sem=sum_send.at[turn, step],
            recv_sem=sum_recv.at[turn, slot],
            device_id=where,
            device_id_type=MESH,
        )

    def wait_sums(turn):
        each(1, reps, lambda step: sum_copy(turn, step, False).wait_recv())
        return jnp.sum(sums[turn], axis=0)[:, :1]

    def back_copy(s, step, sending):
        there, where = block_at(step if sending else blocks - step)
        slot = me if sending else there
        return pltpu.make_async_remote_copy(
            src_ref=back_out.at[s, there],
            dst_ref=back_in.at[s, slot],
            send_sem=back_send.at[s, step],
            recv_sem=back_recv.at[s, slot],
            device_id=where,
            device_id_type=MESH,
        )

    def row_copy(step, sending):
        there, where = block_at(step if sending else blocks - step)
        slot = me if sending else there
        return pltpu.make_async_remote_copy(
            src_ref=outgoing.at[lax.rem(there, groups)],
            dst_ref=arrived.at[slot],
            send_sem=row_send.at[step],
            recv_sem=row_recv.at[slot],
            device_id=where,
            device_id_type=MESH,
        )

    small[0].wait()
    values = tokens_ref[...].astype(F32)
    sums[0, my_r] = jnp.broadcast_to(
        jnp.sum(values * values, axis=1, keepdims=True), (block_tokens, 128)
    )

    wide = blocks * pad
    padded_at = lax.broadcasted_iota(jnp.int32, (wide, slot_rows), 0)
    packed_at = lax.broadcasted_iota(jnp.int32, (wide, slot_rows), 1)
    slot_at = padded_at & (pad - 1)
    spread = (
        (packed_at == (padded_at >> shift) * slot_count + slot_at) & (slot_at < slot_count)
    ).astype(F32).astype(BF16)
    for copy, cot_ref, cot_t in ((small[1], gate_ref, gate_t), (small[2], up_ref, up_t)):
        copy.wait()
        cot_t[...] = lax.dot_general(
            cot_ref[...], spread, (((0,), (1,)), ((), ())), preferred_element_type=F32
        ).astype(BF16)
    for copy in small[3:]:
        copy.wait()
    gain = gain_ref[...].reshape(1, feats)
    code = experts_ref[...] * pad + slots_ref[...]
    code_at = lax.broadcasted_iota(jnp.int32, (groups * pad, block_tokens), 0)
    onehot = ((code[0:1, :] == code_at) | (code[1:2, :] == code_at)).astype(F32)

    inverse_rms = None
    turn = 0
    for s in range(sends):
        total = None
        for k in range(cuts):
            for copy, buf, cot_t in zip(weight_copies(s, k), (gate_buf, up_buf), (gate_t, up_t)):
                copy.wait()
                term = jnp.dot(
                    buf[s, k],
                    cot_t[k * piece : (k + 1) * piece, :],
                    preferred_element_type=F32,
                )
                total = term if total is None else total + term
                turn += 1
                if turn == 1:
                    pl.semaphore_wait(barrier, reps + blocks - 2)
                    each(1, reps, lambda step: sum_copy(0, step, True).start())
                if turn == 2:
                    inverse_rms = lax.rsqrt(wait_sums(0) / model + EPS)
                    scaled_in = values * inverse_rms
                    normed = (scaled_in * gain).astype(BF16)
                    outgoing[...] = (
                        jnp.dot(onehot.astype(BF16), normed, preferred_element_type=F32)
                        .astype(BF16)
                        .reshape(groups, pad, feats)
                    )
                    each(1, blocks, lambda step: row_copy(step, True).start())
                    arrived[me] = outgoing[my_e]
        back_out[s] = total.T.astype(BF16).reshape(blocks, pad, part)
        each(1, blocks, lambda step: back_copy(s, step, True).start())
        back_in[s, me] = back_out[s, me]

    each(1, blocks, lambda step: row_copy(step, False).wait_recv())
    rows_t_ref[...] = lax.dot_general(
        arrived[...].reshape(wide, feats),
        spread,
        (((0,), (0,)), ((), ())),
        preferred_element_type=F32,
    ).astype(BF16)

    pick = jnp.concatenate([onehot] * hids, axis=0).astype(BF16)
    parts = []
    for s in range(sends):
        each(1, blocks, lambda step: back_copy(s, step, False).wait_recv())
        parts.append(
            lax.dot_general(
                pick,
                back_in[s].reshape(wide, part),
                (((0,), (0,)), ((), ())),
                preferred_element_type=F32,
            )
        )
    normed_grad = jnp.concatenate(parts, axis=1)
    scaled = normed_grad * gain
    sums[1, my_r] = jnp.broadcast_to(
        jnp.sum(scaled * scaled_in, axis=1, keepdims=True), (block_tokens, 128)
    )
    each(1, reps, lambda step: sum_copy(1, step, True).start())
    each(1, blocks, lambda step: row_copy(step, True).wait_send())
    for s in range(sends):
        each(1, blocks, lambda step: back_copy(s, step, True).wait_send())
    dotted = wait_sums(1) / model
    grad_tokens_ref[...] = (inverse_rms * (scaled - scaled_in * dotted)).astype(BF16)
    for t in range(2):
        each(1, reps, lambda step: sum_copy(t, step, True).wait_send())


def weight_grad_kernel(
    chunk,
    columns,
    rows_t_hbm,
    gate_hbm,
    up_hbm,
    gate_out,
    up_out,
    rows_t_ref,
    gate_ref,
    up_ref,
    gate_buf,
    up_buf,
    in_sem,
    sem,
):
    inputs = [
        pltpu.make_async_copy(src, dst, in_sem.at[i])
        for i, (src, dst) in enumerate(
            ((rows_t_hbm, rows_t_ref), (gate_hbm, gate_ref), (up_hbm, up_ref))
        )
    ]
    for copy in inputs:
        copy.start()
    for copy in inputs:
        copy.wait()
    feats = rows_t_ref.shape[0]
    width = gate_ref.shape[1]

    def out_copies(c):
        rows = pl.ds(pl.multiple_of(c * chunk, chunk), chunk)
        return (
            pltpu.make_async_copy(gate_buf.at[c], gate_out.at[rows, :], sem.at[0, c]),
            pltpu.make_async_copy(up_buf.at[c], up_out.at[rows, :], sem.at[1, c]),
        )

    def one(c, carry):
        lhs = rows_t_ref[pl.ds(pl.multiple_of(c * chunk, chunk), chunk), :]
        copies = out_copies(c)
        for cot_ref, buf, copy in ((gate_ref, gate_buf, copies[0]), (up_ref, up_buf, copies[1])):
            for at in range(0, width, columns):
                buf[c, :, at : at + columns] = jnp.dot(
                    lhs, cot_ref[:, at : at + columns], preferred_element_type=F32
                ).astype(BF16)
            copy.start()
        return carry

    lax.fori_loop(0, feats // chunk, one, 0)

    def finish(c, carry):
        for copy in out_copies(c):
            copy.wait()
        return carry

    lax.fori_loop(0, feats // chunk, finish, 0)


def on_device(model, tokens, norm_gain, expert_ids, slot_ids, w_gate, w_up, grad_gate, grad_up):
    groups, reps, hids = (lax.axis_size(name) for name in ("expert", "rep", "hid"))
    blocks = groups * hids
    block_tokens, feats = tokens.shape
    slot_count = 5 * block_tokens // (2 * groups)
    pad = max(8, 1 << (slot_count - 1).bit_length())
    width = w_gate.shape[2]
    slot_rows = grad_gate.shape[1]
    chunk = divisor_up_to(feats, 128, 128)
    chunks = feats // chunk
    sends = 2 if feats % 256 == 0 else 1
    part = feats // sends
    piece = divisor_up_to(width, 1024, 128)
    cuts = width // piece
    vmem = pl.BlockSpec(memory_space=pltpu.VMEM)
    hbm = pl.BlockSpec(memory_space=pltpu.HBM)
    wide = blocks * pad
    weight_bytes = feats * width * 2
    gate_cot = grad_gate[0]
    up_cot = grad_up[0]
    rows_t, grad_tokens = pl.pallas_call(
        functools.partial(
            exchange_kernel,
            (groups, reps, hids, slot_count, pad, sends, cuts, model),
        ),
        out_shape=(
            jax.ShapeDtypeStruct((feats, slot_rows), BF16),
            jax.ShapeDtypeStruct((block_tokens, feats), BF16),
        ),
        in_specs=[hbm] * 8,
        out_specs=(vmem, vmem),
        scratch_shapes=[
            pltpu.VMEM((block_tokens, feats), BF16),
            pltpu.VMEM((feats,), F32),
            pltpu.VMEM((2, block_tokens), jnp.int32),
            pltpu.VMEM((2, block_tokens), jnp.int32),
            pltpu.VMEM((slot_rows, width), BF16),
            pltpu.VMEM((slot_rows, width), BF16),
            pltpu.VMEM((sends, cuts, part, piece), BF16),
            pltpu.VMEM((sends, cuts, part, piece), BF16),
            pltpu.VMEM((width, wide), BF16),
            pltpu.VMEM((width, wide), BF16),
            pltpu.VMEM((groups, pad, feats), BF16),
            pltpu.VMEM((blocks, pad, feats), BF16),
            pltpu.VMEM((sends, blocks, pad, part), BF16),
            pltpu.VMEM((sends, blocks, pad, part), BF16),
            pltpu.VMEM((2, reps, block_tokens, 128), F32),
            pltpu.SemaphoreType.DMA((6,)),
            pltpu.SemaphoreType.DMA((2, sends, cuts)),
            pltpu.SemaphoreType.DMA((2, reps)),
            pltpu.SemaphoreType.DMA((2, reps)),
            pltpu.SemaphoreType.DMA((blocks,)),
            pltpu.SemaphoreType.DMA((blocks,)),
            pltpu.SemaphoreType.DMA((sends, blocks)),
            pltpu.SemaphoreType.DMA((sends, blocks)),
        ],
        compiler_params=pltpu.CompilerParams(
            collective_id=0, has_side_effects=True, vmem_limit_bytes=60 * MIB
        ),
        cost_estimate=pl.CostEstimate(
            flops=4 * wide * feats * width,
            bytes_accessed=2 * weight_bytes,
            transcendentals=0,
        ),
        name="rows_and_token_grads",
    )(
        tokens,
        norm_gain,
        expert_ids.T,
        slot_ids.T,
        w_gate[0],
        w_up[0],
        gate_cot,
        up_cot,
    )
    new_gate, new_up = pl.pallas_call(
        functools.partial(weight_grad_kernel, chunk, divisor_up_to(width, 512, 128)),
        out_shape=(
            jax.ShapeDtypeStruct((feats, width), BF16),
            jax.ShapeDtypeStruct((feats, width), BF16),
        ),
        in_specs=[hbm, hbm, hbm],
        out_specs=(hbm, hbm),
        scratch_shapes=[
            pltpu.VMEM((feats, slot_rows), BF16),
            pltpu.VMEM((slot_rows, width), BF16),
            pltpu.VMEM((slot_rows, width), BF16),
            pltpu.VMEM((chunks, chunk, width), BF16),
            pltpu.VMEM((chunks, chunk, width), BF16),
            pltpu.SemaphoreType.DMA((3,)),
            pltpu.SemaphoreType.DMA((2, chunks)),
        ],
        compiler_params=pltpu.CompilerParams(vmem_limit_bytes=60 * MIB),
        cost_estimate=pl.CostEstimate(
            flops=4 * slot_rows * feats * width,
            bytes_accessed=2 * weight_bytes,
            transcendentals=0,
        ),
        name="weight_grads",
    )(rows_t, gate_cot, up_cot)
    return new_gate[None], new_up[None], grad_tokens


def solution(mesh):
    placed = (
        P(("expert", "hid"), "rep"),
        P("rep"),
        P(("expert", "hid"), None),
        P(("expert", "hid"), None),
        P("expert", "rep", "hid"),
        P("expert", "rep", "hid"),
        P("expert", None, "hid"),
        P("expert", None, "hid"),
    )

    def whole(tokens, *rest):
        return jax.shard_map(
            functools.partial(on_device, tokens.shape[1]),
            mesh=mesh,
            in_specs=placed,
            out_specs=(
                P("expert", "rep", "hid"),
                P("expert", "rep", "hid"),
                P(("expert", "hid"), "rep"),
            ),
            check_vma=False,
        )(tokens, *rest)

    return whole
```

```python
import functools

import jax
import jax.numpy as jnp
from jax import lax
from jax.experimental import pallas as pl
from jax.experimental.pallas import tpu as pltpu
from jax.sharding import PartitionSpec as P

EPS = 1e-05
MESH = pl.DeviceIdType.MESH
F32 = jnp.float32
BF16 = jnp.bfloat16
MIB = 1024 * 1024


def divisor_up_to(size, most, step):
    best = size
    for width in range(step, most + 1, step):
        if size % width == 0:
            best = width
    return best


def each(first, last, body):
    if last - first <= 8:
        for step in range(first, last):
            body(step)
    else:

        def go(step, carry):
            body(step)
            return carry

        lax.fori_loop(first, last, go, 0)


def exchange_kernel(
    sizes,
    tokens_hbm,
    gain_hbm,
    experts_hbm,
    slots_hbm,
    w_gate_ref,
    w_up_ref,
    gate_hbm,
    up_hbm,
    rows_t_ref,
    grad_tokens_ref,
    tokens_ref,
    gain_ref,
    experts_ref,
    slots_ref,
    gate_ref,
    up_ref,
    gate_buf,
    up_buf,
    gate_pad,
    up_pad,
    outgoing,
    arrived,
    back_out,
    back_in,
    sums,
    in_sem,
    w_sem,
    sum_send,
    sum_recv,
    row_send,
    row_recv,
    back_send,
    back_recv,
):
    groups, reps, hids, slot_count, pad, chunk, sends, ahead, model = sizes
    blocks = groups * hids
    shift = pad.bit_length() - 1
    my_e = lax.axis_index("expert")
    my_r = lax.axis_index("rep")
    my_h = lax.axis_index("hid")
    me = my_h * groups + my_e
    block_tokens, feats = tokens_ref.shape
    slot_rows = gate_ref.shape[0]
    chunks = feats // chunk
    per_send = chunks // sends
    part = feats // sends

    small = [
        pltpu.make_async_copy(src, dst, in_sem.at[i])
        for i, (src, dst) in enumerate(
            (
                (tokens_hbm, tokens_ref),
                (gate_hbm, gate_ref),
                (up_hbm, up_ref),
                (gain_hbm, gain_ref),
                (experts_hbm, experts_ref),
                (slots_hbm, slots_ref),
            )
        )
    ]
    for copy in small:
        copy.start()

    def weight_copies(c):
        rows = pl.ds(c * chunk, chunk)
        return (
            pltpu.make_async_copy(w_gate_ref.at[rows], gate_buf.at[c], w_sem.at[0, c]),
            pltpu.make_async_copy(w_up_ref.at[rows], up_buf.at[c], w_sem.at[1, c]),
        )

    for c in range(min(ahead, chunks)):
        for copy in weight_copies(c):
            copy.start()

    def block_at(step):
        other = lax.rem(me + step, blocks)
        return other, (lax.rem(other, groups), my_r, lax.div(other, groups))

    def rep_at(step):
        other = lax.rem(my_r + step, reps)
        return other, (my_e, other, my_h)

    if blocks <= 9:
        block_list = [block_at(step) for step in range(blocks)]

        def block_at(step):
            return block_list[step]

    barrier = pltpu.get_barrier_semaphore()
    each(
        1,
        reps,
        lambda step: pl.semaphore_signal(
            barrier, inc=1, device_id=rep_at(step)[1], device_id_type=MESH
        ),
    )
    each(
        1,
        blocks,
        lambda step: pl.semaphore_signal(
            barrier, inc=1, device_id=block_at(step)[1], device_id_type=MESH
        ),
    )

    def sum_copy(turn, step, sending):
        there, where = rep_at(step if sending else reps - step)
        slot = my_r if sending else there
        return pltpu.make_async_remote_copy(
            src_ref=sums.at[turn, my_r],
            dst_ref=sums.at[turn, slot],
            send_sem=sum_send.at[turn, step],
            recv_sem=sum_recv.at[turn, slot],
            device_id=where,
            device_id_type=MESH,
        )

    def wait_sums(turn):
        each(1, reps, lambda step: sum_copy(turn, step, False).wait_recv())
        return jnp.sum(sums[turn], axis=0)[:, :1]

    def back_copy(s, step, sending):
        there, where = block_at(step if sending else blocks - step)
        slot = me if sending else there
        return pltpu.make_async_remote_copy(
            src_ref=back_out.at[s, there],
            dst_ref=back_in.at[s, slot],
            send_sem=back_send.at[s, step],
            recv_sem=back_recv.at[s, slot],
            device_id=where,
            device_id_type=MESH,
        )

    def row_copy(step, sending):
        there, where = block_at(step if sending else blocks - step)
        slot = me if sending else there
        return pltpu.make_async_remote_copy(
            src_ref=outgoing.at[lax.rem(there, groups)],
            dst_ref=arrived.at[slot],
            send_sem=row_send.at[step],
            recv_sem=row_recv.at[slot],
            device_id=where,
            device_id_type=MESH,
        )

    small[0].wait()
    values = tokens_ref[...].astype(F32)
    sums[0, my_r] = jnp.broadcast_to(
        jnp.sum(values * values, axis=1, keepdims=True), (block_tokens, 128)
    )

    wide = blocks * pad
    padded_at = lax.broadcasted_iota(jnp.int32, (wide, slot_rows), 0)
    packed_at = lax.broadcasted_iota(jnp.int32, (wide, slot_rows), 1)
    slot_at = padded_at & (pad - 1)
    spread = (
        (packed_at == (padded_at >> shift) * slot_count + slot_at) & (slot_at < slot_count)
    ).astype(F32).astype(BF16)
    for copy, cot_ref, cot_pad in ((small[1], gate_ref, gate_pad), (small[2], up_ref, up_pad)):
        copy.wait()
        cot_pad[...] = jnp.dot(spread, cot_ref[...], preferred_element_type=F32).astype(BF16)
    for copy in small[3:]:
        copy.wait()
    gain = gain_ref[...].reshape(1, feats)
    code = experts_ref[...] * pad + slots_ref[...]
    code_at = lax.broadcasted_iota(jnp.int32, (groups * pad, block_tokens), 0)
    onehot = ((code[0:1, :] == code_at) | (code[1:2, :] == code_at)).astype(F32)

    for c in range(chunks):
        s, at = c // per_send, c % per_send * chunk
        total = None
        for copy, buf, cot_pad in zip(weight_copies(c), (gate_buf, up_buf), (gate_pad, up_pad)):
            copy.wait()
            if total is None and c + ahead < chunks:
                for later in weight_copies(c + ahead):
                    later.start()
            term = lax.dot_general(
                cot_pad[...], buf[c], (((1,), (1,)), ((), ())), preferred_element_type=F32
            )
            total = term if total is None else total + term
        back_out[s, :, :, at : at + chunk] = total.astype(BF16).reshape(blocks, pad, chunk)
        if c == 0:
            pl.semaphore_wait(barrier, reps + blocks - 2)
            each(1, reps, lambda step: sum_copy(0, step, True).start())
        if at + chunk == part:
            each(1, blocks, lambda step: back_copy(s, step, True).start())
            back_in[s, me] = back_out[s, me]
        if c == chunks * 2 // 3 - 1:
            inverse_rms = lax.rsqrt(wait_sums(0) / model + EPS)
            scaled_in = values * inverse_rms
            normed = (scaled_in * gain).astype(BF16)
            outgoing[...] = (
                jnp.dot(onehot.astype(BF16), normed, preferred_element_type=F32)
                .astype(BF16)
                .reshape(groups, pad, feats)
            )
            each(1, blocks, lambda step: row_copy(step, True).start())
            arrived[me] = outgoing[my_e]

    each(1, blocks, lambda step: row_copy(step, False).wait_recv())
    rows_t_ref[...] = lax.dot_general(
        arrived[...].reshape(wide, feats),
        spread,
        (((0,), (0,)), ((), ())),
        preferred_element_type=F32,
    ).astype(BF16)

    pick = jnp.concatenate([onehot] * hids, axis=0).astype(BF16)
    parts = []
    for s in range(sends):
        each(1, blocks, lambda step: back_copy(s, step, False).wait_recv())
        parts.append(
            lax.dot_general(
                pick,
                back_in[s].reshape(wide, part),
                (((0,), (0,)), ((), ())),
                preferred_element_type=F32,
            )
        )
    normed_grad = jnp.concatenate(parts, axis=1)
    scaled = normed_grad * gain
    sums[1, my_r] = jnp.broadcast_to(
        jnp.sum(scaled * scaled_in, axis=1, keepdims=True), (block_tokens, 128)
    )
    each(1, reps, lambda step: sum_copy(1, step, True).start())
    each(1, blocks, lambda step: row_copy(step, True).wait_send())
    for s in range(sends):
        each(1, blocks, lambda step: back_copy(s, step, True).wait_send())
    dotted = wait_sums(1) / model
    grad_tokens_ref[...] = (inverse_rms * (scaled - scaled_in * dotted)).astype(BF16)
    for t in range(2):
        each(1, reps, lambda step: sum_copy(t, step, True).wait_send())


def weight_grad_kernel(
    chunk,
    columns,
    rows_t_hbm,
    gate_hbm,
    up_hbm,
    tokens_in,
    gate_out,
    up_out,
    tokens_out,
    rows_t_ref,
    gate_ref,
    up_ref,
    gate_buf,
    up_buf,
    in_sem,
    sem,
):
    inputs = [
        pltpu.make_async_copy(src, dst, in_sem.at[i])
        for i, (src, dst) in enumerate(
            (
                (rows_t_hbm, rows_t_ref),
                (gate_hbm, gate_ref),
                (up_hbm, up_ref),
                (tokens_in, tokens_out),
            )
        )
    ]
    for copy in inputs:
        copy.start()
    for copy in inputs[:3]:
        copy.wait()
    feats = rows_t_ref.shape[0]
    width = gate_ref.shape[1]

    def out_copies(c):
        rows = pl.ds(pl.multiple_of(c * chunk, chunk), chunk)
        return (
            pltpu.make_async_copy(gate_buf.at[c], gate_out.at[rows, :], sem.at[0, c]),
            pltpu.make_async_copy(up_buf.at[c], up_out.at[rows, :], sem.at[1, c]),
        )

    def one(c, carry):
        lhs = rows_t_ref[pl.ds(pl.multiple_of(c * chunk, chunk), chunk), :]
        copies = out_copies(c)
        for cot_ref, buf, copy in ((gate_ref, gate_buf, copies[0]), (up_ref, up_buf, copies[1])):
            for at in range(0, width, columns):
                buf[c, :, at : at + columns] = jnp.dot(
                    lhs, cot_ref[:, at : at + columns], preferred_element_type=F32
                ).astype(BF16)
            copy.start()
        return carry

    lax.fori_loop(0, feats // chunk, one, 0)

    def finish(c, carry):
        for copy in out_copies(c):
            copy.wait()
        return carry

    lax.fori_loop(0, feats // chunk, finish, 0)
    inputs[3].wait()


def on_device(model, tokens, norm_gain, expert_ids, slot_ids, w_gate, w_up, grad_gate, grad_up):
    groups, reps, hids = (lax.axis_size(name) for name in ("expert", "rep", "hid"))
    blocks = groups * hids
    block_tokens, feats = tokens.shape
    slot_count = 5 * block_tokens // (2 * groups)
    pad = max(8, 1 << (slot_count - 1).bit_length())
    width = w_gate.shape[2]
    slot_rows = grad_gate.shape[1]
    chunk = divisor_up_to(feats, 256, 128)
    chunks = feats // chunk
    read = divisor_up_to(feats, 256, 128)
    reads = feats // read
    sends = 3 if reads % 3 == 0 else 1
    part = feats // sends
    vmem = pl.BlockSpec(memory_space=pltpu.VMEM)
    hbm = pl.BlockSpec(memory_space=pltpu.HBM)
    wide = blocks * pad
    weight_bytes = feats * width * 2
    gate_cot = grad_gate[0]
    up_cot = grad_up[0]
    rows_t, grad_tokens = pl.pallas_call(
        functools.partial(
            exchange_kernel,
            (groups, reps, hids, slot_count, pad, read, sends, 2, model),
        ),
        out_shape=(
            jax.ShapeDtypeStruct((feats, slot_rows), BF16),
            jax.ShapeDtypeStruct((block_tokens, feats), BF16),
        ),
        in_specs=[hbm] * 8,
        out_specs=(vmem, vmem),
        scratch_shapes=[
            pltpu.VMEM((block_tokens, feats), BF16),
            pltpu.VMEM((feats,), F32),
            pltpu.VMEM((2, block_tokens), jnp.int32),
            pltpu.VMEM((2, block_tokens), jnp.int32),
            pltpu.VMEM((slot_rows, width), BF16),
            pltpu.VMEM((slot_rows, width), BF16),
            pltpu.VMEM((reads, read, width), BF16),
            pltpu.VMEM((reads, read, width), BF16),
            pltpu.VMEM((wide, width), BF16),
            pltpu.VMEM((wide, width), BF16),
            pltpu.VMEM((groups, pad, feats), BF16),
            pltpu.VMEM((blocks, pad, feats), BF16),
            pltpu.VMEM((sends, blocks, pad, part), BF16),
            pltpu.VMEM((sends, blocks, pad, part), BF16),
            pltpu.VMEM((2, reps, block_tokens, 128), F32),
            pltpu.SemaphoreType.DMA((6,)),
            pltpu.SemaphoreType.DMA((2, reads)),
            pltpu.SemaphoreType.DMA((2, reps)),
            pltpu.SemaphoreType.DMA((2, reps)),
            pltpu.SemaphoreType.DMA((blocks,)),
            pltpu.SemaphoreType.DMA((blocks,)),
            pltpu.SemaphoreType.DMA((sends, blocks)),
            pltpu.SemaphoreType.DMA((sends, blocks)),
        ],
        compiler_params=pltpu.CompilerParams(
            collective_id=0, has_side_effects=True, vmem_limit_bytes=60 * MIB
        ),
        cost_estimate=pl.CostEstimate(
            flops=4 * wide * feats * width,
            bytes_accessed=2 * weight_bytes,
            transcendentals=0,
        ),
        name="rows_and_token_grads",
    )(
        tokens,
        norm_gain,
        expert_ids.T,
        slot_ids.T,
        w_gate[0],
        w_up[0],
        gate_cot,
        up_cot,
    )
    new_gate, new_up, new_tokens = pl.pallas_call(
        functools.partial(weight_grad_kernel, chunk, divisor_up_to(width, 512, 128)),
        out_shape=(
            jax.ShapeDtypeStruct((feats, width), BF16),
            jax.ShapeDtypeStruct((feats, width), BF16),
            jax.ShapeDtypeStruct((block_tokens, feats), BF16),
        ),
        in_specs=[hbm] * 4,
        out_specs=(hbm, hbm, hbm),
        scratch_shapes=[
            pltpu.VMEM((feats, slot_rows), BF16),
            pltpu.VMEM((slot_rows, width), BF16),
            pltpu.VMEM((slot_rows, width), BF16),
            pltpu.VMEM((chunks, chunk, width), BF16),
            pltpu.VMEM((chunks, chunk, width), BF16),
            pltpu.SemaphoreType.DMA((4,)),
            pltpu.SemaphoreType.DMA((2, chunks)),
        ],
        compiler_params=pltpu.CompilerParams(vmem_limit_bytes=60 * MIB),
        cost_estimate=pl.CostEstimate(
            flops=4 * slot_rows * feats * width,
            bytes_accessed=2 * weight_bytes,
            transcendentals=0,
        ),
        name="weight_grads",
    )(rows_t, gate_cot, up_cot, grad_tokens)
    return new_gate[None], new_up[None], new_tokens


def solution(mesh):
    placed = (
        P(("expert", "hid"), "rep"),
        P("rep"),
        P(("expert", "hid"), None),
        P(("expert", "hid"), None),
        P("expert", "rep", "hid"),
        P("expert", "rep", "hid"),
        P("expert", None, "hid"),
        P("expert", None, "hid"),
    )

    def whole(tokens, *rest):
        return jax.shard_map(
            functools.partial(on_device, tokens.shape[1]),
            mesh=mesh,
            in_specs=placed,
            out_specs=(
                P("expert", "rep", "hid"),
                P("expert", "rep", "hid"),
                P(("expert", "hid"), "rep"),
            ),
            check_vma=False,
        )(tokens, *rest)

    return whole
```

```python
import functools

import jax
import jax.numpy as jnp
from jax import lax
from jax.experimental import pallas as pl
from jax.experimental.pallas import tpu as pltpu
from jax.sharding import PartitionSpec as P

EPS = 1e-05
MESH = pl.DeviceIdType.MESH
F32 = jnp.float32
BF16 = jnp.bfloat16
MIB = 1024 * 1024


def divisor_up_to(size, most, step):
    best = size
    for width in range(step, most + 1, step):
        if size % width == 0:
            best = width
    return best


def each(first, last, body):
    if last - first <= 8:
        for step in range(first, last):
            body(step)
    else:

        def go(step, carry):
            body(step)
            return carry

        lax.fori_loop(first, last, go, 0)


def exchange_kernel(
    sizes,
    tokens_hbm,
    gain_hbm,
    experts_hbm,
    slots_hbm,
    w_gate_ref,
    gate_hbm,
    up_part_hbm,
    rows_t_ref,
    grad_tokens_ref,
    tokens_ref,
    gain_ref,
    experts_ref,
    slots_ref,
    gate_ref,
    up_part_ref,
    gate_buf,
    gate_pad,
    up_pad,
    outgoing,
    arrived,
    back_out,
    back_in,
    sums,
    in_sem,
    w_sem,
    sum_send,
    sum_recv,
    row_send,
    row_recv,
    back_send,
    back_recv,
):
    groups, reps, hids, slot_count, pad, chunk, sends, ahead, model = sizes
    blocks = groups * hids
    shift = pad.bit_length() - 1
    my_e = lax.axis_index("expert")
    my_r = lax.axis_index("rep")
    my_h = lax.axis_index("hid")
    me = my_h * groups + my_e
    block_tokens, feats = tokens_ref.shape
    slot_rows = gate_ref.shape[0]
    chunks = feats // chunk
    per_send = chunks // sends
    part = feats // sends

    small = [
        pltpu.make_async_copy(src, dst, in_sem.at[i])
        for i, (src, dst) in enumerate(
            (
                (tokens_hbm, tokens_ref),
                (gate_hbm, gate_ref),
                (up_part_hbm, up_part_ref),
                (gain_hbm, gain_ref),
                (experts_hbm, experts_ref),
                (slots_hbm, slots_ref),
            )
        )
    ]
    for copy in small:
        copy.start()

    def weight_copy(c):
        return pltpu.make_async_copy(
            w_gate_ref.at[pl.ds(c * chunk, chunk)], gate_buf.at[c], w_sem.at[c]
        )

    for c in range(min(ahead, chunks)):
        weight_copy(c).start()

    def block_at(step):
        other = lax.rem(me + step, blocks)
        return other, (lax.rem(other, groups), my_r, lax.div(other, groups))

    def rep_at(step):
        other = lax.rem(my_r + step, reps)
        return other, (my_e, other, my_h)

    if blocks <= 9:
        block_list = [block_at(step) for step in range(blocks)]

        def block_at(step):
            return block_list[step]

    barrier = pltpu.get_barrier_semaphore()
    each(
        1,
        reps,
        lambda step: pl.semaphore_signal(
            barrier, inc=1, device_id=rep_at(step)[1], device_id_type=MESH
        ),
    )
    each(
        1,
        blocks,
        lambda step: pl.semaphore_signal(
            barrier, inc=1, device_id=block_at(step)[1], device_id_type=MESH
        ),
    )

    def sum_copy(turn, step, sending):
        there, where = rep_at(step if sending else reps - step)
        slot = my_r if sending else there
        return pltpu.make_async_remote_copy(
            src_ref=sums.at[turn, my_r],
            dst_ref=sums.at[turn, slot],
            send_sem=sum_send.at[turn, step],
            recv_sem=sum_recv.at[turn, slot],
            device_id=where,
            device_id_type=MESH,
        )

    def wait_sums(turn):
        each(1, reps, lambda step: sum_copy(turn, step, False).wait_recv())
        return jnp.sum(sums[turn], axis=0)[:, :1]

    def back_copy(s, step, sending):
        there, where = block_at(step if sending else blocks - step)
        slot = me if sending else there
        return pltpu.make_async_remote_copy(
            src_ref=back_out.at[s, there],
            dst_ref=back_in.at[s, slot],
            send_sem=back_send.at[s, step],
            recv_sem=back_recv.at[s, slot],
            device_id=where,
            device_id_type=MESH,
        )

    def row_copy(step, sending):
        there, where = block_at(step if sending else blocks - step)
        slot = me if sending else there
        return pltpu.make_async_remote_copy(
            src_ref=outgoing.at[lax.rem(there, groups)],
            dst_ref=arrived.at[slot],
            send_sem=row_send.at[step],
            recv_sem=row_recv.at[slot],
            device_id=where,
            device_id_type=MESH,
        )

    small[0].wait()
    values = tokens_ref[...].astype(F32)
    sums[0, my_r] = jnp.broadcast_to(
        jnp.sum(values * values, axis=1, keepdims=True), (block_tokens, 128)
    )

    wide = blocks * pad
    padded_at = lax.broadcasted_iota(jnp.int32, (wide, slot_rows), 0)
    packed_at = lax.broadcasted_iota(jnp.int32, (wide, slot_rows), 1)
    slot_at = padded_at & (pad - 1)
    spread = (
        (packed_at == (padded_at >> shift) * slot_count + slot_at) & (slot_at < slot_count)
    ).astype(F32).astype(BF16)
    small[1].wait()
    gate_pad[...] = jnp.dot(spread, gate_ref[...], preferred_element_type=F32).astype(BF16)
    small[2].wait()
    up_part = up_part_ref[...]
    leading = up_part.astype(BF16)
    rest = (up_part - leading.astype(F32)).astype(BF16)
    up_pad[...] = jnp.dot(spread, leading, preferred_element_type=F32) + jnp.dot(
        spread, rest, preferred_element_type=F32
    )
    for copy in small[3:]:
        copy.wait()
    gain = gain_ref[...].reshape(1, feats)
    code = experts_ref[...] * pad + slots_ref[...]
    code_at = lax.broadcasted_iota(jnp.int32, (groups * pad, block_tokens), 0)
    onehot = ((code[0:1, :] == code_at) | (code[1:2, :] == code_at)).astype(F32)

    for c in range(chunks):
        s, at = c // per_send, c % per_send * chunk
        weight_copy(c).wait()
        if c + ahead < chunks:
            weight_copy(c + ahead).start()
        total = up_pad[:, c * chunk : (c + 1) * chunk] + lax.dot_general(
            gate_pad[...], gate_buf[c], (((1,), (1,)), ((), ())), preferred_element_type=F32
        )
        back_out[s, :, :, at : at + chunk] = total.astype(BF16).reshape(blocks, pad, chunk)
        if c == 0:
            pl.semaphore_wait(barrier, reps + blocks - 2)
            each(1, reps, lambda step: sum_copy(0, step, True).start())
        if at + chunk == part:
            each(1, blocks, lambda step: back_copy(s, step, True).start())
            back_in[s, me] = back_out[s, me]
        if c == max(chunks * 2 // 3 - 1, 0):
            inverse_rms = lax.rsqrt(wait_sums(0) / model + EPS)
            scaled_in = values * inverse_rms
            normed = (scaled_in * gain).astype(BF16)
            outgoing[...] = (
                jnp.dot(onehot.astype(BF16), normed, preferred_element_type=F32)
                .astype(BF16)
                .reshape(groups, pad, feats)
            )
            each(1, blocks, lambda step: row_copy(step, True).start())
            arrived[me] = outgoing[my_e]

    each(1, blocks, lambda step: row_copy(step, False).wait_recv())
    rows_t_ref[...] = lax.dot_general(
        arrived[...].reshape(wide, feats),
        spread,
        (((0,), (0,)), ((), ())),
        preferred_element_type=F32,
    ).astype(BF16)

    pick = jnp.concatenate([onehot] * hids, axis=0).astype(BF16)
    parts = []
    for s in range(sends):
        each(1, blocks, lambda step: back_copy(s, step, False).wait_recv())
        parts.append(
            lax.dot_general(
                pick,
                back_in[s].reshape(wide, part),
                (((0,), (0,)), ((), ())),
                preferred_element_type=F32,
            )
        )
    normed_grad = jnp.concatenate(parts, axis=1)
    scaled = normed_grad * gain
    sums[1, my_r] = jnp.broadcast_to(
        jnp.sum(scaled * scaled_in, axis=1, keepdims=True), (block_tokens, 128)
    )
    each(1, reps, lambda step: sum_copy(1, step, True).start())
    each(1, blocks, lambda step: row_copy(step, True).wait_send())
    for s in range(sends):
        each(1, blocks, lambda step: back_copy(s, step, True).wait_send())
    dotted = wait_sums(1) / model
    grad_tokens_ref[...] = (inverse_rms * (scaled - scaled_in * dotted)).astype(BF16)
    for t in range(2):
        each(1, reps, lambda step: sum_copy(t, step, True).wait_send())


def weight_grad_kernel(
    chunk,
    columns,
    rows_t_hbm,
    gate_hbm,
    up_hbm,
    tokens_in,
    gate_out,
    up_out,
    tokens_out,
    rows_t_ref,
    gate_ref,
    up_ref,
    gate_buf,
    up_buf,
    in_sem,
    sem,
):
    inputs = [
        pltpu.make_async_copy(src, dst, in_sem.at[i])
        for i, (src, dst) in enumerate(
            (
                (rows_t_hbm, rows_t_ref),
                (gate_hbm, gate_ref),
                (up_hbm, up_ref),
                (tokens_in, tokens_out),
            )
        )
    ]
    for copy in inputs:
        copy.start()
    for copy in inputs[:3]:
        copy.wait()
    feats = rows_t_ref.shape[0]
    width = gate_ref.shape[1]

    def out_copies(c):
        rows = pl.ds(pl.multiple_of(c * chunk, chunk), chunk)
        return (
            pltpu.make_async_copy(gate_buf.at[c], gate_out.at[rows, :], sem.at[0, c]),
            pltpu.make_async_copy(up_buf.at[c], up_out.at[rows, :], sem.at[1, c]),
        )

    def one(c, carry):
        lhs = rows_t_ref[pl.ds(pl.multiple_of(c * chunk, chunk), chunk), :]
        copies = out_copies(c)
        for cot_ref, buf, copy in ((gate_ref, gate_buf, copies[0]), (up_ref, up_buf, copies[1])):
            for at in range(0, width, columns):
                buf[c, :, at : at + columns] = jnp.dot(
                    lhs, cot_ref[:, at : at + columns], preferred_element_type=F32
                ).astype(BF16)
            copy.start()
        return carry

    lax.fori_loop(0, feats // chunk, one, 0)

    def finish(c, carry):
        for copy in out_copies(c):
            copy.wait()
        return carry

    lax.fori_loop(0, feats // chunk, finish, 0)
    inputs[3].wait()


def on_device(model, tokens, norm_gain, expert_ids, slot_ids, w_gate, w_up, grad_gate, grad_up):
    groups, reps, hids = (lax.axis_size(name) for name in ("expert", "rep", "hid"))
    blocks = groups * hids
    block_tokens, feats = tokens.shape
    slot_count = 5 * block_tokens // (2 * groups)
    pad = max(8, 1 << (slot_count - 1).bit_length())
    width = w_gate.shape[2]
    slot_rows = grad_gate.shape[1]
    chunk = divisor_up_to(feats, 256, 128)
    chunks = feats // chunk
    read = divisor_up_to(feats, 512, 128)
    reads = feats // read
    sends = 3 if reads % 3 == 0 else 1
    part = feats // sends
    vmem = pl.BlockSpec(memory_space=pltpu.VMEM)
    hbm = pl.BlockSpec(memory_space=pltpu.HBM)
    wide = blocks * pad
    weight_bytes = feats * width * 2
    gate_cot = grad_gate[0]
    up_cot = grad_up[0]
    up_part = lax.dot_general(
        up_cot, w_up[0], (((1,), (1,)), ((), ())), preferred_element_type=F32
    )
    rows_t, grad_tokens = pl.pallas_call(
        functools.partial(
            exchange_kernel,
            (groups, reps, hids, slot_count, pad, read, sends, 2, model),
        ),
        out_shape=(
            jax.ShapeDtypeStruct((feats, slot_rows), BF16),
            jax.ShapeDtypeStruct((block_tokens, feats), BF16),
        ),
        in_specs=[hbm] * 7,
        out_specs=(vmem, vmem),
        scratch_shapes=[
            pltpu.VMEM((block_tokens, feats), BF16),
            pltpu.VMEM((feats,), F32),
            pltpu.VMEM((2, block_tokens), jnp.int32),
            pltpu.VMEM((2, block_tokens), jnp.int32),
            pltpu.VMEM((slot_rows, width), BF16),
            pltpu.VMEM((slot_rows, feats), F32),
            pltpu.VMEM((reads, read, width), BF16),
            pltpu.VMEM((wide, width), BF16),
            pltpu.VMEM((wide, feats), F32),
            pltpu.VMEM((groups, pad, feats), BF16),
            pltpu.VMEM((blocks, pad, feats), BF16),
            pltpu.VMEM((sends, blocks, pad, part), BF16),
            pltpu.VMEM((sends, blocks, pad, part), BF16),
            pltpu.VMEM((2, reps, block_tokens, 128), F32),
            pltpu.SemaphoreType.DMA((6,)),
            pltpu.SemaphoreType.DMA((reads,)),
            pltpu.SemaphoreType.DMA((2, reps)),
            pltpu.SemaphoreType.DMA((2, reps)),
            pltpu.SemaphoreType.DMA((blocks,)),
            pltpu.SemaphoreType.DMA((blocks,)),
            pltpu.SemaphoreType.DMA((sends, blocks)),
            pltpu.SemaphoreType.DMA((sends, blocks)),
        ],
        compiler_params=pltpu.CompilerParams(
            collective_id=0, has_side_effects=True, vmem_limit_bytes=60 * MIB
        ),
        cost_estimate=pl.CostEstimate(
            flops=2 * wide * feats * width,
            bytes_accessed=weight_bytes,
            transcendentals=0,
        ),
        name="rows_and_token_grads",
    )(
        tokens,
        norm_gain,
        expert_ids.T,
        slot_ids.T,
        w_gate[0],
        gate_cot,
        up_part,
    )
    new_gate, new_up, new_tokens = pl.pallas_call(
        functools.partial(weight_grad_kernel, chunk, divisor_up_to(width, 512, 128)),
        out_shape=(
            jax.ShapeDtypeStruct((feats, width), BF16),
            jax.ShapeDtypeStruct((feats, width), BF16),
            jax.ShapeDtypeStruct((block_tokens, feats), BF16),
        ),
        in_specs=[hbm] * 4,
        out_specs=(hbm, hbm, hbm),
        scratch_shapes=[
            pltpu.VMEM((feats, slot_rows), BF16),
            pltpu.VMEM((slot_rows, width), BF16),
            pltpu.VMEM((slot_rows, width), BF16),
            pltpu.VMEM((chunks, chunk, width), BF16),
            pltpu.VMEM((chunks, chunk, width), BF16),
            pltpu.SemaphoreType.DMA((4,)),
            pltpu.SemaphoreType.DMA((2, chunks)),
        ],
        compiler_params=pltpu.CompilerParams(vmem_limit_bytes=60 * MIB),
        cost_estimate=pl.CostEstimate(
            flops=4 * slot_rows * feats * width,
            bytes_accessed=2 * weight_bytes,
            transcendentals=0,
        ),
        name="weight_grads",
    )(rows_t, gate_cot, up_cot, grad_tokens)
    return new_gate[None], new_up[None], new_tokens


def solution(mesh):
    placed = (
        P(("expert", "hid"), "rep"),
        P("rep"),
        P(("expert", "hid"), None),
        P(("expert", "hid"), None),
        P("expert", "rep", "hid"),
        P("expert", "rep", "hid"),
        P("expert", None, "hid"),
        P("expert", None, "hid"),
    )

    def whole(tokens, *rest):
        return jax.shard_map(
            functools.partial(on_device, tokens.shape[1]),
            mesh=mesh,
            in_specs=placed,
            out_specs=(
                P("expert", "rep", "hid"),
                P("expert", "rep", "hid"),
                P(("expert", "hid"), "rep"),
            ),
            check_vma=False,
        )(tokens, *rest)

    return whole
```

```python
import functools

import jax
import jax.numpy as jnp
from jax import lax
from jax.experimental import pallas as pl
from jax.experimental.pallas import tpu as pltpu
from jax.sharding import PartitionSpec as P

EPS = 1e-05
MESH = pl.DeviceIdType.MESH
F32 = jnp.float32
BF16 = jnp.bfloat16
MIB = 1024 * 1024


def divisor_up_to(size, most, step):
    best = size
    for width in range(step, most + 1, step):
        if size % width == 0:
            best = width
    return best


def each(first, last, body):
    if last - first <= 8:
        for step in range(first, last):
            body(step)
    else:

        def go(step, carry):
            body(step)
            return carry

        lax.fori_loop(first, last, go, 0)


def exchange_kernel(
    sizes,
    tokens_hbm,
    gain_hbm,
    experts_hbm,
    slots_hbm,
    partial_hbm,
    rows_t_ref,
    grad_tokens_ref,
    tokens_ref,
    gain_ref,
    experts_ref,
    slots_ref,
    partial_ref,
    outgoing,
    arrived,
    back_out,
    back_in,
    sums,
    in_sem,
    sum_send,
    sum_recv,
    row_send,
    row_recv,
    back_send,
    back_recv,
):
    groups, reps, hids, slot_count, pad, sends, model = sizes
    blocks = groups * hids
    shift = pad.bit_length() - 1
    my_e = lax.axis_index("expert")
    my_r = lax.axis_index("rep")
    my_h = lax.axis_index("hid")
    me = my_h * groups + my_e
    block_tokens, feats = tokens_ref.shape
    slot_rows = partial_ref.shape[0]
    part = feats // sends

    small = [
        pltpu.make_async_copy(src, dst, in_sem.at[i])
        for i, (src, dst) in enumerate(
            (
                (tokens_hbm, tokens_ref),
                (partial_hbm, partial_ref),
                (gain_hbm, gain_ref),
                (experts_hbm, experts_ref),
                (slots_hbm, slots_ref),
            )
        )
    ]
    for copy in small:
        copy.start()

    def block_at(step):
        other = lax.rem(me + step, blocks)
        return other, (lax.rem(other, groups), my_r, lax.div(other, groups))

    def rep_at(step):
        other = lax.rem(my_r + step, reps)
        return other, (my_e, other, my_h)

    if blocks <= 9:
        block_list = [block_at(step) for step in range(blocks)]

        def block_at(step):
            return block_list[step]

    barrier = pltpu.get_barrier_semaphore()
    each(
        1,
        reps,
        lambda step: pl.semaphore_signal(
            barrier, inc=1, device_id=rep_at(step)[1], device_id_type=MESH
        ),
    )
    each(
        1,
        blocks,
        lambda step: pl.semaphore_signal(
            barrier, inc=1, device_id=block_at(step)[1], device_id_type=MESH
        ),
    )

    def sum_copy(turn, step, sending):
        there, where = rep_at(step if sending else reps - step)
        slot = my_r if sending else there
        return pltpu.make_async_remote_copy(
            src_ref=sums.at[turn, my_r],
            dst_ref=sums.at[turn, slot],
            send_sem=sum_send.at[turn, step],
            recv_sem=sum_recv.at[turn, slot],
            device_id=where,
            device_id_type=MESH,
        )

    def wait_sums(turn):
        each(1, reps, lambda step: sum_copy(turn, step, False).wait_recv())
        return jnp.sum(sums[turn], axis=0)[:, :1]

    def back_copy(s, step, sending):
        there, where = block_at(step if sending else blocks - step)
        slot = me if sending else there
        return pltpu.make_async_remote_copy(
            src_ref=back_out.at[s, there],
            dst_ref=back_in.at[s, slot],
            send_sem=back_send.at[s, step],
            recv_sem=back_recv.at[s, slot],
            device_id=where,
            device_id_type=MESH,
        )

    def row_copy(step, sending):
        there, where = block_at(step if sending else blocks - step)
        slot = me if sending else there
        return pltpu.make_async_remote_copy(
            src_ref=outgoing.at[lax.rem(there, groups)],
            dst_ref=arrived.at[slot],
            send_sem=row_send.at[step],
            recv_sem=row_recv.at[slot],
            device_id=where,
            device_id_type=MESH,
        )

    small[0].wait()
    values = tokens_ref[...].astype(F32)
    sums[0, my_r] = jnp.broadcast_to(
        jnp.sum(values * values, axis=1, keepdims=True), (block_tokens, 128)
    )

    wide = blocks * pad
    padded_at = lax.broadcasted_iota(jnp.int32, (wide, slot_rows), 0)
    packed_at = lax.broadcasted_iota(jnp.int32, (wide, slot_rows), 1)
    slot_at = padded_at & (pad - 1)
    spread = (
        (packed_at == (padded_at >> shift) * slot_count + slot_at) & (slot_at < slot_count)
    ).astype(F32).astype(BF16)
    small[1].wait()
    back_out[0] = (
        jnp.dot(spread, partial_ref[...].astype(BF16), preferred_element_type=F32)
        .astype(BF16)
        .reshape(blocks, pad, feats)
    )
    for copy in small[2:]:
        copy.wait()
    gain = gain_ref[...].reshape(1, feats)
    code = experts_ref[...] * pad + slots_ref[...]
    code_at = lax.broadcasted_iota(jnp.int32, (groups * pad, block_tokens), 0)
    onehot = ((code[0:1, :] == code_at) | (code[1:2, :] == code_at)).astype(F32)

    pl.semaphore_wait(barrier, reps + blocks - 2)
    each(1, reps, lambda step: sum_copy(0, step, True).start())
    each(1, blocks, lambda step: back_copy(0, step, True).start())
    back_in[0, me] = back_out[0, me]
    inverse_rms = lax.rsqrt(wait_sums(0) / model + EPS)
    scaled_in = values * inverse_rms
    normed = (scaled_in * gain).astype(BF16)
    outgoing[...] = (
        jnp.dot(onehot.astype(BF16), normed, preferred_element_type=F32)
        .astype(BF16)
        .reshape(groups, pad, feats)
    )
    each(1, blocks, lambda step: row_copy(step, True).start())
    arrived[me] = outgoing[my_e]

    each(1, blocks, lambda step: row_copy(step, False).wait_recv())
    rows_t_ref[...] = lax.dot_general(
        arrived[...].reshape(wide, feats),
        spread,
        (((0,), (0,)), ((), ())),
        preferred_element_type=F32,
    ).astype(BF16)

    pick = jnp.concatenate([onehot] * hids, axis=0).astype(BF16)
    parts = []
    for s in range(sends):
        each(1, blocks, lambda step: back_copy(s, step, False).wait_recv())
        parts.append(
            lax.dot_general(
                pick,
                back_in[s].reshape(wide, part),
                (((0,), (0,)), ((), ())),
                preferred_element_type=F32,
            )
        )
    normed_grad = jnp.concatenate(parts, axis=1)
    scaled = normed_grad * gain
    sums[1, my_r] = jnp.broadcast_to(
        jnp.sum(scaled * scaled_in, axis=1, keepdims=True), (block_tokens, 128)
    )
    each(1, reps, lambda step: sum_copy(1, step, True).start())
    each(1, blocks, lambda step: row_copy(step, True).wait_send())
    for s in range(sends):
        each(1, blocks, lambda step: back_copy(s, step, True).wait_send())
    dotted = wait_sums(1) / model
    grad_tokens_ref[...] = (inverse_rms * (scaled - scaled_in * dotted)).astype(BF16)
    for t in range(2):
        each(1, reps, lambda step: sum_copy(t, step, True).wait_send())


def weight_grad_kernel(
    chunk,
    columns,
    rows_t_hbm,
    gate_hbm,
    up_hbm,
    tokens_in,
    gate_out,
    up_out,
    tokens_out,
    rows_t_ref,
    gate_ref,
    up_ref,
    gate_buf,
    up_buf,
    in_sem,
    sem,
):
    inputs = [
        pltpu.make_async_copy(src, dst, in_sem.at[i])
        for i, (src, dst) in enumerate(
            (
                (rows_t_hbm, rows_t_ref),
                (gate_hbm, gate_ref),
                (up_hbm, up_ref),
                (tokens_in, tokens_out),
            )
        )
    ]
    for copy in inputs:
        copy.start()
    for copy in inputs[:3]:
        copy.wait()
    feats = rows_t_ref.shape[0]
    width = gate_ref.shape[1]

    def out_copies(c):
        rows = pl.ds(pl.multiple_of(c * chunk, chunk), chunk)
        return (
            pltpu.make_async_copy(gate_buf.at[c], gate_out.at[rows, :], sem.at[0, c]),
            pltpu.make_async_copy(up_buf.at[c], up_out.at[rows, :], sem.at[1, c]),
        )

    def one(c, carry):
        lhs = rows_t_ref[pl.ds(pl.multiple_of(c * chunk, chunk), chunk), :]
        copies = out_copies(c)
        for cot_ref, buf, copy in ((gate_ref, gate_buf, copies[0]), (up_ref, up_buf, copies[1])):
            for at in range(0, width, columns):
                buf[c, :, at : at + columns] = jnp.dot(
                    lhs, cot_ref[:, at : at + columns], preferred_element_type=F32
                ).astype(BF16)
            copy.start()
        return carry

    lax.fori_loop(0, feats // chunk, one, 0)

    def finish(c, carry):
        for copy in out_copies(c):
            copy.wait()
        return carry

    lax.fori_loop(0, feats // chunk, finish, 0)
    inputs[3].wait()


def on_device(model, tokens, norm_gain, expert_ids, slot_ids, w_gate, w_up, grad_gate, grad_up):
    groups, reps, hids = (lax.axis_size(name) for name in ("expert", "rep", "hid"))
    blocks = groups * hids
    block_tokens, feats = tokens.shape
    slot_count = 5 * block_tokens // (2 * groups)
    pad = max(8, 1 << (slot_count - 1).bit_length())
    width = w_gate.shape[2]
    slot_rows = grad_gate.shape[1]
    chunk = divisor_up_to(feats, 256, 128)
    chunks = feats // chunk
    sends = 1
    part = feats
    vmem = pl.BlockSpec(memory_space=pltpu.VMEM)
    hbm = pl.BlockSpec(memory_space=pltpu.HBM)
    wide = blocks * pad
    weight_bytes = feats * width * 2
    gate_cot = grad_gate[0]
    up_cot = grad_up[0]
    unit_contract = (((1,), (1,)), ((), ()))
    partial = lax.dot_general(
        gate_cot, w_gate[0], unit_contract, preferred_element_type=F32
    ) + lax.dot_general(up_cot, w_up[0], unit_contract, preferred_element_type=F32)
    rows_t, grad_tokens = pl.pallas_call(
        functools.partial(
            exchange_kernel,
            (groups, reps, hids, slot_count, pad, sends, model),
        ),
        out_shape=(
            jax.ShapeDtypeStruct((feats, slot_rows), BF16),
            jax.ShapeDtypeStruct((block_tokens, feats), BF16),
        ),
        in_specs=[hbm] * 5,
        out_specs=(vmem, vmem),
        scratch_shapes=[
            pltpu.VMEM((block_tokens, feats), BF16),
            pltpu.VMEM((feats,), F32),
            pltpu.VMEM((2, block_tokens), jnp.int32),
            pltpu.VMEM((2, block_tokens), jnp.int32),
            pltpu.VMEM((slot_rows, feats), F32),
            pltpu.VMEM((groups, pad, feats), BF16),
            pltpu.VMEM((blocks, pad, feats), BF16),
            pltpu.VMEM((sends, blocks, pad, part), BF16),
            pltpu.VMEM((sends, blocks, pad, part), BF16),
            pltpu.VMEM((2, reps, block_tokens, 128), F32),
            pltpu.SemaphoreType.DMA((6,)),
            pltpu.SemaphoreType.DMA((2, reps)),
            pltpu.SemaphoreType.DMA((2, reps)),
            pltpu.SemaphoreType.DMA((blocks,)),
            pltpu.SemaphoreType.DMA((blocks,)),
            pltpu.SemaphoreType.DMA((sends, blocks)),
            pltpu.SemaphoreType.DMA((sends, blocks)),
        ],
        compiler_params=pltpu.CompilerParams(
            collective_id=0, has_side_effects=True, vmem_limit_bytes=24 * MIB
        ),
        cost_estimate=pl.CostEstimate(
            flops=4 * wide * wide * feats,
            bytes_accessed=8 * wide * feats,
            transcendentals=0,
        ),
        name="rows_and_token_grads",
    )(
        tokens,
        norm_gain,
        expert_ids.T,
        slot_ids.T,
        partial,
    )
    new_gate, new_up, new_tokens = pl.pallas_call(
        functools.partial(weight_grad_kernel, chunk, divisor_up_to(width, 512, 128)),
        out_shape=(
            jax.ShapeDtypeStruct((feats, width), BF16),
            jax.ShapeDtypeStruct((feats, width), BF16),
            jax.ShapeDtypeStruct((block_tokens, feats), BF16),
        ),
        in_specs=[hbm] * 4,
        out_specs=(hbm, hbm, hbm),
        scratch_shapes=[
            pltpu.VMEM((feats, slot_rows), BF16),
            pltpu.VMEM((slot_rows, width), BF16),
            pltpu.VMEM((slot_rows, width), BF16),
            pltpu.VMEM((chunks, chunk, width), BF16),
            pltpu.VMEM((chunks, chunk, width), BF16),
            pltpu.SemaphoreType.DMA((4,)),
            pltpu.SemaphoreType.DMA((2, chunks)),
        ],
        compiler_params=pltpu.CompilerParams(vmem_limit_bytes=36 * MIB),
        cost_estimate=pl.CostEstimate(
            flops=4 * slot_rows * feats * width,
            bytes_accessed=2 * weight_bytes,
            transcendentals=0,
        ),
        name="weight_grads",
    )(rows_t, gate_cot, up_cot, grad_tokens)
    return new_gate[None], new_up[None], new_tokens


def solution(mesh):
    placed = (
        P(("expert", "hid"), "rep"),
        P("rep"),
        P(("expert", "hid"), None),
        P(("expert", "hid"), None),
        P("expert", "rep", "hid"),
        P("expert", "rep", "hid"),
        P("expert", None, "hid"),
        P("expert", None, "hid"),
    )

    def whole(tokens, *rest):
        return jax.shard_map(
            functools.partial(on_device, tokens.shape[1]),
            mesh=mesh,
            in_specs=placed,
            out_specs=(
                P("expert", "rep", "hid"),
                P("expert", "rep", "hid"),
                P(("expert", "hid"), "rep"),
            ),
            check_vma=False,
        )(tokens, *rest)

    return whole
```
